32 devices in a mesh: groups: 2 (over x), gx: 16 (over z, y, core).
Axes of the slice: x: 2, y: 2, z: 4, core: 2. Of those that a mesh axis runs over, the one named last changes fastest.
Arguments:
- terminal: float32 [32, 128, 2048], P('groups', 'gx'), parts along dimension 0, may hold values from -6 to 6
- misfit: float32 [4, 32, 128, 2048], P(None, 'groups', 'gx'), parts along dimension 1, may hold values from -6 to 6
- material: int32 [16, 128, 16], P(None, 'gx'), may hold values from 0 to 7
- material_table: float32 [2, 8], replicated, may hold values from 0.3 to 1
- heater_slot: int32 [8192], replicated, may hold values from 0 to 8191, as said below
- entry_heater: int32 [32768], P('gx'), may hold values from 0 to 8191, as said below
- entry_block: int32 [32768], P('gx'), may hold values from 0 to 2047
- profile: float32 [32768, 128], P('gx'), may hold values from -0.5 to 0.5
Outputs:
- adjoint: float32 [32, 128, 2048], P('groups', 'gx'), parts along dimension 0
- heater_grad: float32 [16384], P(('groups', 'gx')), parts along dimension 0
The draws below stay inside these ranges and needn't reach their ends.
There are 2 independent parts, one for each index of `groups`. The reference program is written for one: setup_inputs(seed, part) draws one part's arguments, and reference() takes and returns one part's arrays. A program takes and returns all parts, laid end to end along the dimension named above; an argument that names none is the same for every part. Nothing has to cross between parts.
Inputs may be any that keep to these rules, and one draw needn't show every extreme that they name: heater_slot is a permutation of the slots. `entry_heater`: among one device's 2048 entries, at most 256 have heaters whose slots lie on any one owning device, and on each device exactly 256 go to some owner.
All inputs are finite; a program needn't handle non-finite values.
Results may differ from the reference program's by a relative error of at most 0.00002.
Values sent between devices are 32-bit elements; how exact they have to be, the bound alone decides.
A program may use at most 64 MiB of HBM per device.

```python
import math
import jax
import jax.numpy as jnp

NZ = 16
CX = 8
NY = 2048
STEPS = 4
BLOCK = 128
MATS = 8
HEAT_DEV = 512
ENT_DEV = 2048
NX = 128
NYB = 16
BLOCKS_DEV = 2048
HEATERS = 8192
ENTRIES = 32768
CAP = 256
N_GX = 16


def shared_slots(key):
    return jax.random.permutation(key, HEATERS).astype(jnp.int32)


def draw_heater_slot(key, part):
    return shared_slots(key)


def draw_entry_heater(key, part):
    slot_table = shared_slots(key)
    heater_of_slot = jnp.argsort(slot_table).astype(jnp.int32)
    key = jax.random.fold_in(key, 7)
    total = N_GX * CAP

    def one_device(device_key):
        first, second, third = jax.random.split(device_key, 3)
        filled = jax.random.randint(first, (), 0, N_GX, dtype=jnp.int32)
        places = jnp.arange(total, dtype=jnp.int32)
        scores = jax.random.randint(second, (total,), 0, 16384, dtype=jnp.int32) * total + places
        scores = scores + jnp.where(places // CAP == filled, 0, 536870912).astype(jnp.int32)
        chosen = jnp.argsort(scores)[:ENT_DEV].astype(jnp.int32)
        owners = chosen // CAP
        within = jax.random.randint(third, (ENT_DEV,), 0, HEAT_DEV, dtype=jnp.int32)
        return heater_of_slot[owners * HEAT_DEV + within]
    device_keys = jax.vmap(lambda index: jax.random.fold_in(key, index))(jnp.arange(N_GX, dtype=jnp.int32))
    return jax.vmap(one_device)(device_keys).reshape(-1).astype(jnp.int32)


def with_ends(values, own_key, low, largest):
    dims = values.shape
    index_at = [jax.random.randint(jax.random.fold_in(own_key, axis), (), 0, dims[axis]) for axis in range(len(dims))]
    values = values.at[tuple(index_at)].set(low)
    longest = dims.index(max(dims))
    index_at[longest] = (index_at[longest] + 1) % dims[longest]
    return values.at[tuple(index_at)].set(largest)


def block_scale(stream_key, extent, cuts, least, largest):
    def one(dim, blocks):
        draws = jax.random.uniform(jax.random.fold_in(jax.random.fold_in(stream_key, 6), dim), (blocks,), jnp.float32, least / len(cuts), largest / len(cuts))
        return jnp.repeat(jnp.exp(draws), extent[dim] // blocks).reshape((-1,) + (1,) * (len(extent) - dim - 1))

    loudness = one(*cuts[0])
    for cut in cuts[1:]:
        loudness = loudness * one(*cut)
    return loudness


def gaussian(stream_key, shape, spread, bound, pieces=(), held_as=jnp.bfloat16):
    gain = block_scale(stream_key, shape, pieces, -0.22, 0.18) if pieces else 1.0
    array = jax.random.normal(stream_key, shape, jnp.float32) * spread * gain
    return jnp.minimum(jnp.maximum(array, -bound), bound).astype(held_as)


def setup_inputs(seed: int = 0, part: int = 0) -> dict:
    keys = jax.random.split(jax.random.key(seed), 9)
    part_keys = jax.random.split(jax.random.fold_in(keys[8], part), 9)
    terminal = gaussian(part_keys[0], (NZ, NX, NY), 1.0, 6.0, ((1, 16),), jnp.float32)
    misfit = gaussian(part_keys[1], (STEPS, NZ, NX, NY), 1.0, 6.0, ((2, 16),), jnp.float32)
    material = with_ends(jax.random.randint(keys[2], (NZ, NX, NYB), 0, MATS), jax.random.fold_in(keys[2], 1), 0, MATS - 1).astype(jnp.int32)
    material_table = jnp.clip(jnp.exp(jax.random.uniform(keys[3], (2, MATS), jnp.float32, math.log(0.3), math.log(1.0))), 0.3, 1.0)
    heater_slot = draw_heater_slot(jax.random.fold_in(keys[8], 71), part)
    entry_heater = draw_entry_heater(jax.random.fold_in(keys[8], 71), part)
    entry_block = with_ends(jax.random.randint(keys[6], (ENTRIES,), 0, BLOCKS_DEV), jax.random.fold_in(keys[6], 1), 0, BLOCKS_DEV - 1).astype(jnp.int32)
    profile = gaussian(keys[7], (ENTRIES, BLOCK), BLOCK ** -0.5, 0.5, ((0, 16),), jnp.float32)
    return dict(terminal=terminal, misfit=misfit, material=material, material_table=material_table, heater_slot=heater_slot, entry_heater=entry_heater, entry_block=entry_block, profile=profile)


def operate(field, lateral, vertical, inside_x):
    center = field[:, 1:-1]
    own_lat = lateral[:, 1:-1]
    own_vert = vertical[:, 1:-1]
    summed = jnp.zeros_like(center)
    for lower, upper in ((2, None), (0, -2)):
        conductance = 0.5 * (own_lat + lateral[:, lower:upper]) * inside_x[:, lower:upper]
        summed = summed + conductance * (field[:, lower:upper] - center)
    edges = ((0, 0), (0, 0), (1, 1))
    field_y = jnp.pad(center, edges)
    lat_y = jnp.pad(own_lat, edges)
    open_y = jnp.pad(jnp.ones((1, 1, center.shape[2]), jnp.float32), edges)
    for lower, upper in ((2, None), (0, -2)):
        conductance = 0.5 * (own_lat + lat_y[:, :, lower:upper]) * open_y[:, :, lower:upper]
        summed = summed + conductance * (field_y[:, :, lower:upper] - center)
    edges_z = ((1, 1), (0, 0), (0, 0))
    field_z = jnp.pad(center, edges_z)
    vert_z = jnp.pad(own_vert, edges_z)
    open_z = jnp.pad(jnp.ones((center.shape[0], 1, 1), jnp.float32), edges_z)
    for lower, upper in ((2, None), (0, -2)):
        conductance = 0.5 * (own_vert + vert_z[lower:upper]) * open_z[lower:upper]
        summed = summed + conductance * (field_z[lower:upper] - center)
    return summed


def reference(terminal, misfit, material, material_table, heater_slot, entry_heater, entry_block, profile):
    time_step = 0.16
    matches = material[..., None] == jnp.arange(MATS, dtype=jnp.int32)
    blocked = jnp.sum(jnp.where(matches[None], material_table[:, None, None, None, :], 0.0), axis=-1)
    cells = jnp.repeat(blocked, BLOCK, axis=3)
    edges_x = ((0, 0), (0, 0), (1, 1), (0, 0))
    cells = jnp.pad(cells, edges_x)
    inside_x = jnp.pad(jnp.ones((1, NX, 1), jnp.float32), ((0, 0), (1, 1), (0, 0)))
    field = terminal
    accumulated = jnp.zeros_like(terminal)
    for step_index in range(STEPS):
        extended = jnp.pad(field, ((0, 0), (1, 1), (0, 0)))
        field = field + time_step * operate(extended, cells[0], cells[1], inside_x) + misfit[step_index]
        accumulated = accumulated + field
    entries = jnp.arange(ENTRIES, dtype=jnp.int32)
    device = entries // ENT_DEV
    layer = entry_block // (CX * NYB)
    column = (entry_block // NYB) % CX
    yblock = entry_block % NYB
    flat = layer * (NX * NYB) + (device * CX + column) * NYB + yblock
    picked = accumulated.reshape(-1, BLOCK)[flat]
    values = time_step * jnp.sum(picked * profile, axis=1)
    slots = heater_slot[entry_heater]
    heater_grad = jnp.zeros((HEATERS,), jnp.float32).at[slots].add(values)
    return field, heater_grad
```

```python
import functools

import jax
import jax.numpy as jnp
from jax import lax
from jax.experimental import pallas as pl
from jax.experimental.pallas import tpu as pltpu
from jax.sharding import PartitionSpec as P

MESH = pl.DeviceIdType.MESH
DT = 0.16
LANES = 128


def ceil8(rows):
    return (rows + 7) // 8 * 8


def kernel(
    n, layers, across, nyb, steps, mats, per_owner,
    term, misfit, mat, table, slot_table, heaters, block, profile,
    adjoint, grad,
    fields, mis, prof, gxp, gxm, gyp, gym, gz, c0, packed, vpacked, total, picked,
    one_lo, one_hi, dense, send_lo, send_hi, from_lo, from_hi, parts,
    sem_term, sem_mis, sem_prof, sem_out, send_sems, recv_sems, out_sems, in_sems,
):
    me = lax.axis_index("gx")
    slab = nyb * across
    rows = layers * slab
    edge = nyb * layers
    table_rows = slot_table.shape[0]
    entries = heaters.shape[0] * LANES
    owner_rows = per_owner // LANES
    pad_rows = ceil8(owner_rows)

    barrier = pltpu.get_barrier_semaphore()

    def greet(d, _):
        pl.semaphore_signal(
            barrier, inc=1, device_id={"gx": lax.rem(me + d, n)}, device_id_type=MESH
        )
        return 0

    lax.fori_loop(1, n, greet, 0)

    load_term = pltpu.make_async_copy(term, fields.at[0, pl.ds(slab, rows)], sem_term)
    load_term.start()
    loads = [
        pltpu.make_async_copy(misfit.at[t], mis.at[t], sem_mis.at[t]) for t in range(steps)
    ]
    for load in loads:
        load.start()
    load_prof = pltpu.make_async_copy(profile, prof, sem_prof)
    load_prof.start()

    sub = lax.broadcasted_iota(jnp.int32, (across, LANES), 0)
    lane = lax.broadcasted_iota(jnp.int32, (across, LANES), 1)
    lane_e = lax.broadcasted_iota(jnp.int32, (layers, LANES), 1)

    index = mat[...]
    lat = jnp.zeros(index.shape, jnp.float32)
    ver = jnp.zeros(index.shape, jnp.float32)
    for m in range(mats):
        lat = jnp.where(index == m, table[0, m], lat)
        ver = jnp.where(index == m, table[1, m], ver)
    packed[...] = jnp.zeros(packed.shape, jnp.float32)
    vpacked[...] = jnp.zeros(vpacked.shape, jnp.float32)
    packed[:, pl.ds(0, nyb)] = lat
    vpacked[:, pl.ds(0, nyb)] = ver

    zeros_slab = jnp.zeros((slab, LANES), jnp.float32)
    for t in range(steps):
        fields[t, pl.ds(0, slab), :] = zeros_slab
        fields[t, pl.ds(slab + rows, slab), :] = zeros_slab
    gz[pl.ds(0, slab), :] = zeros_slab
    gz[pl.ds(rows, slab), :] = zeros_slab

    @pl.when(me == 0)
    def _():
        from_lo[...] = jnp.zeros(from_lo.shape, jnp.float32)

    @pl.when(me == n - 1)
    def _():
        from_hi[...] = jnp.zeros(from_hi.shape, jnp.float32)

    def hop(t, up):
        count = edge + layers if t == 0 else edge
        s = 1 if up else 0
        return pltpu.make_async_remote_copy(
            src_ref=(send_hi if up else send_lo).at[t, pl.ds(0, count)],
            dst_ref=(from_lo if up else from_hi).at[t, pl.ds(0, count)],
            send_sem=send_sems.at[t, s],
            recv_sem=recv_sems.at[t, s],
            device_id={"gx": me + 1 if up else me - 1},
            device_id_type=MESH,
        )

    def send(t):
        @pl.when(me < n - 1)
        def _():
            hop(t, True).start()

        @pl.when(me > 0)
        def _():
            hop(t, False).start()

    def receive(t):
        @pl.when(me > 0)
        def _():
            hop(t, True).wait_recv()

        @pl.when(me < n - 1)
        def _():
            hop(t, False).wait_recv()

    load_term.wait()
    for s, (buffer, x) in enumerate(((send_lo, 0), (send_hi, across - 1))):
        for b in range(nyb):
            buffer[0, pl.ds(b * layers, layers), :] = fields[
                0, pl.ds(slab + b * across + x, layers, stride=slab), :
            ]
        buffer[0, pl.ds(edge, layers), :] = packed[pl.ds(x, layers, stride=across), :]
    pl.semaphore_wait(barrier, n - 1)
    send(0)

    half = 0.5 * DT

    def coefficients(k, _):
        at = pl.multiple_of(k * across, across)
        base = pl.multiple_of(k * slab, slab)
        lat = packed[pl.ds(at, across), :]
        ver = vpacked[pl.ds(at, across), :]
        upper = jnp.minimum(k + 1, layers - 1)
        ver_up = vpacked[pl.ds(pl.multiple_of(upper * across, across), across), :]
        lower = jnp.maximum(k - 1, 0)
        ver_down = vpacked[pl.ds(pl.multiple_of(lower * across, across), across), :]
        z_up = jnp.where(k < layers - 1, half, 0.0) * (ver + ver_up)
        z_down = jnp.where(k > 0, half, 0.0) * (ver + ver_down)
        x_up = half * (lat + pltpu.roll(lat, across - 1, 0))
        x_down = half * (lat + pltpu.roll(lat, 1, 0))
        side = half * (lat + pltpu.roll(lat, LANES - 1, 1))
        inner = DT * lat
        center = 1.0 - z_up - z_down

        def wide(value, b):
            return jnp.broadcast_to(value[:, b : b + 1], (across, LANES))

        none = jnp.zeros((across, LANES), jnp.float32)
        sides = [none] + [wide(side, b) for b in range(nyb - 1)] + [none]
        for b in range(nyb):
            own = pl.ds(base + b * across, across)
            y = wide(inner, b)
            y_up = jnp.where(lane == LANES - 1, sides[b + 1], y)
            y_down = jnp.where(lane == 0, sides[b], y)
            gyp[own, :] = y_up
            gym[own, :] = y_down
            gxp[own, :] = wide(x_up, b)
            gxm[own, :] = wide(x_down, b)
            gz[pl.ds(base + slab + b * across, across), :] = wide(z_up, b)
            c0[own, :] = wide(center, b) - y_up - y_down
        return 0

    lax.fori_loop(0, layers, coefficients, 0)

    cut = 4
    width = cut * LANES
    slots = slot_table[...]
    pieces = jnp.concatenate(
        [
            jnp.right_shift(slots, 8).astype(jnp.float32).T,
            jnp.bitwise_and(slots, 255).astype(jnp.float32).T,
        ],
        axis=0,
    ).astype(jnp.bfloat16)

    def lookup(c, _):
        heater = jnp.concatenate(
            [heaters[pl.ds(c * cut + j, 1), :] for j in range(cut)], axis=1
        )
        high = (
            lax.broadcasted_iota(jnp.int32, (table_rows, width), 0)
            == jnp.right_shift(heater, 7)
        ).astype(jnp.float32).astype(jnp.bfloat16)
        found = jnp.dot(pieces, high, preferred_element_type=jnp.float32)
        lanes = lax.broadcasted_iota(jnp.int32, (LANES, width), 0)
        mine = lanes == jnp.bitwise_and(heater, LANES - 1)
        big = jnp.sum(jnp.where(mine, found[:LANES], 0.0), axis=0, keepdims=True)
        small = jnp.sum(jnp.where(mine, found[LANES:], 0.0), axis=0, keepdims=True)
        slot = (big * 256.0 + small).astype(jnp.int32)
        owner = slot // per_owner
        place = owner * pad_rows + (slot - owner * per_owner) // LANES
        one_hi[:, pl.ds(pl.multiple_of(c * width, width), width)] = (
            lax.broadcasted_iota(jnp.int32, (n * pad_rows, width), 0) == place
        ).astype(jnp.float32).astype(jnp.bfloat16)
        low = (lanes == jnp.bitwise_and(slot, LANES - 1)).astype(jnp.float32)
        for j in range(cut):
            one_lo[pl.ds(pl.multiple_of(c * width, width) + j * LANES, LANES), :] = low[
                :, j * LANES : (j + 1) * LANES
            ].T
        return 0

    lookups = entries // width
    lax.fori_loop(0, lookups, lookup, 0)

    receive(0)
    for x, ref, arrived, outside in (
        (0, gxm, from_lo, me == 0),
        (across - 1, gxp, from_hi, me == n - 1),
    ):
        scale = jnp.where(outside, 0.0, half)
        pair = scale * (
            packed[pl.ds(x, layers, stride=across), :] + arrived[0, pl.ds(edge, layers), :]
        )
        for b in range(nyb):
            ref[pl.ds(b * across + x, layers, stride=slab), :] = jnp.broadcast_to(
                pair[:, b : b + 1], (layers, LANES)
            )

    def edges(t):
        for x, inward, g_in, g_out, arrived, buffer in (
            (0, 1, gxp, gxm, from_lo, send_lo),
            (across - 1, -1, gxm, gxp, from_hi, send_hi),
        ):
            def at(ref, b, shift=0):
                return ref[pl.ds(shift + b * across + x, layers, stride=slab), :]

            def at_f(b, shift):
                return fields[t, pl.ds(shift + b * across + x, layers, stride=slab), :]

            v = [at_f(b, slab) for b in range(nyb)]
            right = [pltpu.roll(u, LANES - 1, 1) for u in v]
            left = [pltpu.roll(u, 1, 1) for u in v]
            for b in range(nyb):
                y_up = jnp.where(lane_e == LANES - 1, right[min(b + 1, nyb - 1)], right[b])
                y_down = jnp.where(lane_e == 0, left[max(b - 1, 0)], left[b])
                here = v[b]
                inner = at_f(b, slab + inward)
                outer = arrived[t, pl.ds(b * layers, layers), :]
                new = (
                    (at(c0, b) * here + at(gyp, b) * y_up)
                    + (at(gym, b) * y_down + at(g_in, b) * (inner - here))
                ) + (
                    (at(g_out, b) * (outer - here) + at(gz, b, slab) * at_f(b, 2 * slab))
                    + (at(gz, b) * at_f(b, 0)
                       + mis[t, pl.ds(b * across + x, layers, stride=slab), :])
                )
                buffer[t + 1, pl.ds(b * layers, layers), :] = new

    def interior(t, last):
        def body(k, _):
            base = pl.multiple_of(k * slab, slab)
            v = [fields[t, pl.ds(base + slab + b * across, across), :] for b in range(nyb)]
            right = [pltpu.roll(u, LANES - 1, 1) for u in v]
            left = [pltpu.roll(u, 1, 1) for u in v]
            for b in range(nyb):
                own = pl.ds(base + b * across, across)
                here = v[b]
                y_up = jnp.where(lane == LANES - 1, right[min(b + 1, nyb - 1)], right[b])
                y_down = jnp.where(lane == 0, left[max(b - 1, 0)], left[b])
                x_up = jnp.where(
                    sub == across - 1,
                    from_hi[t, pl.ds(b * layers + k, 1), :],
                    pltpu.roll(here, across - 1, 0),
                )
                x_down = jnp.where(
                    sub == 0, from_lo[t, pl.ds(b * layers + k, 1), :], pltpu.roll(here, 1, 0)
                )
                z_up = fields[t, pl.ds(base + 2 * slab + b * across, across), :]
                z_down = fields[t, own, :]
                new = (
                    (c0[own, :] * here + gyp[own, :] * y_up)
                    + (gym[own, :] * y_down + gxp[own, :] * (x_up - here))
                ) + (
                    (gxm[own, :] * (x_down - here)
                     + gz[pl.ds(base + slab + b * across, across), :] * z_up)
                    + (gz[own, :] * z_down + mis[t, own, :])
                )
                if last:
                    picked[own, :] = new
                    acc = new
                    for s in range(1, steps):
                        acc = acc + fields[s, pl.ds(base + slab + b * across, across), :]
                    total[pl.ds(base + b, across, stride=nyb), :] = acc
                else:
                    fields[t + 1, pl.ds(base + slab + b * across, across), :] = new
            return 0

        lax.fori_loop(0, layers, body, 0)

    for t in range(steps):
        last = t == steps - 1
        loads[t].wait()
        if t > 0:
            receive(t)
        if not last:
            edges(t)
            send(t + 1)
        interior(t, last)

    store = pltpu.make_async_copy(picked.at[pl.ds(0, rows)], adjoint, sem_out)
    store.start()
    load_prof.wait()

    unroll = 32

    def pick(c, _):
        base = pl.multiple_of(c * unroll, unroll)
        for j in range(unroll):
            picked[pl.ds(rows + base + j, 1), :] = total[pl.ds(block[base + j], 1), :]
        return 0

    lax.fori_loop(0, entries // unroll, pick, 0)

    chunk = 512
    sums = jnp.zeros((n * pad_rows, 3 * LANES), jnp.float32)
    for c in range(entries // chunk):
        own = pl.ds(c * chunk, chunk)
        value = DT * jnp.sum(
            picked[pl.ds(rows + c * chunk, chunk), :] * prof[own, :], axis=1, keepdims=True
        )
        spread = one_lo[own, :] * value
        first = spread.astype(jnp.bfloat16)
        rest = spread - first.astype(jnp.float32)
        second = rest.astype(jnp.bfloat16)
        third = (rest - second.astype(jnp.float32)).astype(jnp.bfloat16)
        sums = sums + jnp.dot(
            one_hi[:, c * chunk : (c + 1) * chunk],
            jnp.concatenate([first, second, third], axis=1),
            preferred_element_type=jnp.float32,
        )
    dense[...] = (
        (sums[:, 2 * LANES :] + sums[:, LANES : 2 * LANES]) + sums[:, :LANES]
    ).reshape(n, pad_rows, LANES)

    def deliver(d):
        peer = lax.rem(me + d, n)
        return pltpu.make_async_remote_copy(
            src_ref=dense.at[peer],
            dst_ref=parts.at[d],
            send_sem=out_sems.at[d],
            recv_sem=in_sems.at[d],
            device_id={"gx": peer},
            device_id_type=MESH,
        )

    def start(d, _):
        deliver(d).start()
        return 0

    lax.fori_loop(1, n, start, 0)

    for t in range(steps):
        @pl.when(me < n - 1)
        def _():
            hop(t, True).wait_send()

        @pl.when(me > 0)
        def _():
            hop(t, False).wait_send()

    store.wait()

    def finish(d, acc):
        deliver(d).wait_recv()
        return acc + parts[d]

    result = lax.fori_loop(1, n, finish, dense[me])
    grad[...] = result[:owner_rows]

    def drain(d, _):
        deliver(d).wait_send()
        return 0

    lax.fori_loop(1, n, drain, 0)


def on_device(
    terminal, misfit, material, material_table, heater_slot, entry_heater, entry_block, profile
):
    n = lax.axis_size("gx")
    layers, across, depth = terminal.shape
    steps = misfit.shape[0]
    mats = material_table.shape[1]
    nyb = depth // LANES
    entries = entry_block.shape[0]
    per_owner = heater_slot.shape[0] // n
    rows, slab, edge = layers * across * nyb, across * nyb, layers * nyb
    pad_rows = ceil8(per_owner // LANES)
    term = terminal.reshape(layers, across, nyb, LANES).swapaxes(1, 2).reshape(rows, LANES)
    mis = (
        misfit.reshape(steps, layers, across, nyb, LANES).swapaxes(2, 3).reshape(steps, rows, LANES)
    )
    any_space = pl.BlockSpec(memory_space=pl.ANY)
    vmem = pl.BlockSpec(memory_space=pltpu.VMEM)
    smem = pl.BlockSpec(memory_space=pltpu.SMEM)
    f32 = jnp.float32
    adjoint, grad = pl.pallas_call(
        functools.partial(kernel, n, layers, across, nyb, steps, mats, per_owner),
        out_shape=(
            jax.ShapeDtypeStruct((rows, LANES), f32),
            jax.ShapeDtypeStruct((per_owner // LANES, LANES), f32),
        ),
        in_specs=[any_space, any_space, vmem, smem, vmem, vmem, smem, any_space],
        out_specs=(any_space, vmem),
        scratch_shapes=[
            pltpu.VMEM((steps, rows + 2 * slab, LANES), f32),
            pltpu.VMEM((steps, rows, LANES), f32),
            pltpu.VMEM((entries, LANES), f32),
            pltpu.VMEM((rows, LANES), f32),
            pltpu.VMEM((rows, LANES), f32),
            pltpu.VMEM((rows, LANES), f32),
            pltpu.VMEM((rows, LANES), f32),
            pltpu.VMEM((rows + slab, LANES), f32),
            pltpu.VMEM((rows, LANES), f32),
            pltpu.VMEM((layers * across, LANES), f32),
            pltpu.VMEM((layers * across, LANES), f32),
            pltpu.VMEM((rows, LANES), f32),
            pltpu.VMEM((rows + entries, LANES), f32),
            pltpu.VMEM((entries, LANES), f32),
            pltpu.VMEM((n * pad_rows, entries), jnp.bfloat16),
            pltpu.VMEM((n, pad_rows, LANES), f32),
            pltpu.VMEM((steps, edge + layers, LANES), f32),
            pltpu.VMEM((steps, edge + layers, LANES), f32),
            pltpu.VMEM((steps, edge + layers, LANES), f32),
            pltpu.VMEM((steps, edge + layers, LANES), f32),
            pltpu.VMEM((n, pad_rows, LANES), f32),
            pltpu.SemaphoreType.DMA,
            pltpu.SemaphoreType.DMA((steps,)),
            pltpu.SemaphoreType.DMA,
            pltpu.SemaphoreType.DMA,
            pltpu.SemaphoreType.DMA((steps, 2)),
            pltpu.SemaphoreType.DMA((steps, 2)),
            pltpu.SemaphoreType.DMA((n,)),
            pltpu.SemaphoreType.DMA((n,)),
        ],
        compiler_params=pltpu.CompilerParams(
            collective_id=0, has_side_effects=True, vmem_limit_bytes=48 * 1024 * 1024
        ),
    )(
        term,
        mis,
        material.reshape(layers * across, nyb),
        material_table,
        heater_slot.reshape(-1, LANES),
        entry_heater.reshape(-1, LANES),
        entry_block,
        profile,
    )
    adjoint = adjoint.reshape(layers, nyb, across, LANES).swapaxes(1, 2).reshape(terminal.shape)
    return (adjoint, grad.reshape(per_owner))


def solution(mesh):
    return jax.shard_map(
        on_device,
        mesh=mesh,
        in_specs=(
            P("groups", "gx", None),
            P(None, "groups", "gx", None),
            P(None, "gx", None),
            P(),
            P(),
            P("gx"),
            P("gx"),
            P("gx", None),
        ),
        out_specs=(P("groups", "gx", None), P(("groups", "gx"))),
        check_vma=False,
    )
```

```python
import functools

import jax
import jax.numpy as jnp
from jax import lax
from jax.experimental import pallas as pl
from jax.experimental.pallas import tpu as pltpu
from jax.sharding import PartitionSpec as P

MESH = pl.DeviceIdType.MESH
DT = 0.16
LANES = 128


def ceil8(rows):
    return (rows + 7) // 8 * 8


def kernel(
    n, layers, across, nyb, steps, mats, per_owner,
    term, misfit, mat_hbm, table_hbm, slots_hbm, heaters_hbm, block_hbm, profile,
    adjoint, grad,
    mat, table, slot_table, heaters, block,
    fields, mis, prof, gxp, gxm, gyp, gym, gz, c0, packed, vpacked, total, picked,
    one_lo, one_hi, dense, send_lo, send_hi, from_lo, from_hi, parts,
    sem_term, sem_mis, sem_prof, sem_small, send_sems, recv_sems, out_sems, in_sems,
):
    me = lax.axis_index("gx")
    slab = nyb * across
    rows = layers * slab
    edge = nyb * layers
    table_rows = slot_table.shape[0]
    entries = heaters.shape[0] * LANES
    owner_rows = per_owner // LANES
    pad_rows = ceil8(owner_rows)

    barrier = pltpu.get_barrier_semaphore()

    def greet(d, _):
        pl.semaphore_signal(
            barrier, inc=1, device_id={"gx": lax.rem(me + d, n)}, device_id_type=MESH
        )
        return 0

    lax.fori_loop(1, n, greet, 0)

    small = [
        pltpu.make_async_copy(source, target, sem_small.at[i])
        for i, (source, target) in enumerate((
            (mat_hbm, mat), (table_hbm, table), (slots_hbm, slot_table),
            (heaters_hbm, heaters), (block_hbm, block),
        ))
    ]
    for load in small:
        load.start()
    load_term = pltpu.make_async_copy(term, fields.at[0, pl.ds(slab, rows)], sem_term)
    load_term.start()
    loads = [
        pltpu.make_async_copy(misfit.at[t], mis.at[t], sem_mis.at[t]) for t in range(steps)
    ]
    for load in loads:
        load.start()
    load_prof = pltpu.make_async_copy(profile, prof, sem_prof)
    load_prof.start()

    sub = lax.broadcasted_iota(jnp.int32, (across, LANES), 0)
    lane = lax.broadcasted_iota(jnp.int32, (across, LANES), 1)
    lane_e = lax.broadcasted_iota(jnp.int32, (layers, LANES), 1)

    small[0].wait()
    small[1].wait()
    index = mat[...]
    lat = jnp.zeros(index.shape, jnp.float32)
    ver = jnp.zeros(index.shape, jnp.float32)
    for m in range(mats):
        lat = jnp.where(index == m, table[0, m], lat)
        ver = jnp.where(index == m, table[1, m], ver)
    packed[...] = jnp.zeros(packed.shape, jnp.float32)
    vpacked[...] = jnp.zeros(vpacked.shape, jnp.float32)
    packed[:, pl.ds(0, nyb)] = lat
    vpacked[:, pl.ds(0, nyb)] = ver

    zeros_slab = jnp.zeros((slab, LANES), jnp.float32)
    for t in range(steps):
        fields[t, pl.ds(0, slab), :] = zeros_slab
        fields[t, pl.ds(slab + rows, slab), :] = zeros_slab
    gz[pl.ds(0, slab), :] = zeros_slab
    gz[pl.ds(rows, slab), :] = zeros_slab

    @pl.when(me == 0)
    def _():
        from_lo[...] = jnp.zeros(from_lo.shape, jnp.float32)

    @pl.when(me == n - 1)
    def _():
        from_hi[...] = jnp.zeros(from_hi.shape, jnp.float32)

    def hop(t, up):
        count = edge + layers if t == 0 else edge
        s = 1 if up else 0
        return pltpu.make_async_remote_copy(
            src_ref=(send_hi if up else send_lo).at[t, pl.ds(0, count)],
            dst_ref=(from_lo if up else from_hi).at[t, pl.ds(0, count)],
            send_sem=send_sems.at[t, s],
            recv_sem=recv_sems.at[t, s],
            device_id={"gx": me + 1 if up else me - 1},
            device_id_type=MESH,
        )

    def send(t):
        @pl.when(me < n - 1)
        def _():
            hop(t, True).start()

        @pl.when(me > 0)
        def _():
            hop(t, False).start()

    def receive(t):
        @pl.when(me > 0)
        def _():
            hop(t, True).wait_recv()

        @pl.when(me < n - 1)
        def _():
            hop(t, False).wait_recv()

    load_term.wait()
    for s, (buffer, x) in enumerate(((send_lo, 0), (send_hi, across - 1))):
        for b in range(nyb):
            buffer[0, pl.ds(b * layers, layers), :] = fields[
                0, pl.ds(slab + b * across + x, layers, stride=slab), :
            ]
        buffer[0, pl.ds(edge, layers), :] = packed[pl.ds(x, layers, stride=across), :]
    pl.semaphore_wait(barrier, n - 1)
    send(0)

    half = 0.5 * DT

    def coefficients(k, _):
        at = pl.multiple_of(k * across, across)
        base = pl.multiple_of(k * slab, slab)
        lat = packed[pl.ds(at, across), :]
        ver = vpacked[pl.ds(at, across), :]
        upper = jnp.minimum(k + 1, layers - 1)
        ver_up = vpacked[pl.ds(pl.multiple_of(upper * across, across), across), :]
        lower = jnp.maximum(k - 1, 0)
        ver_down = vpacked[pl.ds(pl.multiple_of(lower * across, across), across), :]
        z_up = jnp.where(k < layers - 1, half, 0.0) * (ver + ver_up)
        z_down = jnp.where(k > 0, half, 0.0) * (ver + ver_down)
        x_up = half * (lat + pltpu.roll(lat, across - 1, 0))
        x_down = half * (lat + pltpu.roll(lat, 1, 0))
        side = half * (lat + pltpu.roll(lat, LANES - 1, 1))
        inner = DT * lat
        center = 1.0 - z_up - z_down

        def wide(value, b):
            return jnp.broadcast_to(value[:, b : b + 1], (across, LANES))

        none = jnp.zeros((across, LANES), jnp.float32)
        sides = [none] + [wide(side, b) for b in range(nyb - 1)] + [none]
        for b in range(nyb):
            own = pl.ds(base + b * across, across)
            y = wide(inner, b)
            y_up = jnp.where(lane == LANES - 1, sides[b + 1], y)
            y_down = jnp.where(lane == 0, sides[b], y)
            gyp[own, :] = y_up
            gym[own, :] = y_down
            gxp[own, :] = wide(x_up, b)
            gxm[own, :] = wide(x_down, b)
            gz[pl.ds(base + slab + b * across, across), :] = wide(z_up, b)
            c0[own, :] = wide(center, b) - y_up - y_down
        return 0

    lax.fori_loop(0, layers, coefficients, 0)

    for load in small[2:]:
        load.wait()
    cut = 4
    width = cut * LANES
    slots = slot_table[...]
    pieces = jnp.concatenate(
        [
            jnp.right_shift(slots, 8).astype(jnp.float32).T,
            jnp.bitwise_and(slots, 255).astype(jnp.float32).T,
        ],
        axis=0,
    ).astype(jnp.bfloat16)

    def lookup(c, _):
        heater = jnp.concatenate(
            [heaters[pl.ds(c * cut + j, 1), :] for j in range(cut)], axis=1
        )
        high = (
            lax.broadcasted_iota(jnp.int32, (table_rows, width), 0)
            == jnp.right_shift(heater, 7)
        ).astype(jnp.float32).astype(jnp.bfloat16)
        found = jnp.dot(pieces, high, preferred_element_type=jnp.float32)
        lanes = lax.broadcasted_iota(jnp.int32, (LANES, width), 0)
        mine = lanes == jnp.bitwise_and(heater, LANES - 1)
        big = jnp.sum(jnp.where(mine, found[:LANES], 0.0), axis=0, keepdims=True)
        small = jnp.sum(jnp.where(mine, found[LANES:], 0.0), axis=0, keepdims=True)
        slot = (big * 256.0 + small).astype(jnp.int32)
        owner = slot // per_owner
        place = owner * pad_rows + (slot - owner * per_owner) // LANES
        one_hi[:, pl.ds(pl.multiple_of(c * width, width), width)] = (
            lax.broadcasted_iota(jnp.int32, (n * pad_rows, width), 0) == place
        ).astype(jnp.float32).astype(jnp.bfloat16)
        low = (lanes == jnp.bitwise_and(slot, LANES - 1)).astype(jnp.float32)
        for j in range(cut):
            one_lo[pl.ds(pl.multiple_of(c * width, width) + j * LANES, LANES), :] = low[
                :, j * LANES : (j + 1) * LANES
            ].T
        return 0

    lookups = entries // width
    lax.fori_loop(0, lookups, lookup, 0)

    receive(0)
    for x, ref, arrived, outside in (
        (0, gxm, from_lo, me == 0),
        (across - 1, gxp, from_hi, me == n - 1),
    ):
        scale = jnp.where(outside, 0.0, half)
        pair = scale * (
            packed[pl.ds(x, layers, stride=across), :] + arrived[0, pl.ds(edge, layers), :]
        )
        for b in range(nyb):
            ref[pl.ds(b * across + x, layers, stride=slab), :] = jnp.broadcast_to(
                pair[:, b : b + 1], (layers, LANES)
            )

    def edges(t):
        for x, inward, g_in, g_out, arrived, buffer in (
            (0, 1, gxp, gxm, from_lo, send_lo),
            (across - 1, -1, gxm, gxp, from_hi, send_hi),
        ):
            def at(ref, b, shift=0):
                return ref[pl.ds(shift + b * across + x, layers, stride=slab), :]

            def at_f(b, shift):
                return fields[t, pl.ds(shift + b * across + x, layers, stride=slab), :]

            v = [at_f(b, slab) for b in range(nyb)]
            right = [pltpu.roll(u, LANES - 1, 1) for u in v]
            left = [pltpu.roll(u, 1, 1) for u in v]
            for b in range(nyb):
                y_up = jnp.where(lane_e == LANES - 1, right[min(b + 1, nyb - 1)], right[b])
                y_down = jnp.where(lane_e == 0, left[max(b - 1, 0)], left[b])
                here = v[b]
                inner = at_f(b, slab + inward)
                outer = arrived[t, pl.ds(b * layers, layers), :]
                new = (
                    (at(c0, b) * here + at(gyp, b) * y_up)
                    + (at(gym, b) * y_down + at(g_in, b) * (inner - here))
                ) + (
                    (at(g_out, b) * (outer - here) + at(gz, b, slab) * at_f(b, 2 * slab))
                    + (at(gz, b) * at_f(b, 0)
                       + mis[t, pl.ds(b * across + x, layers, stride=slab), :])
                )
                buffer[t + 1, pl.ds(b * layers, layers), :] = new

    def interior(t, last):
        def body(k, _):
            base = pl.multiple_of(k * slab, slab)
            v = [fields[t, pl.ds(base + slab + b * across, across), :] for b in range(nyb)]
            right = [pltpu.roll(u, LANES - 1, 1) for u in v]
            left = [pltpu.roll(u, 1, 1) for u in v]
            for b in range(nyb):
                own = pl.ds(base + b * across, across)
                here = v[b]
                y_up = jnp.where(lane == LANES - 1, right[min(b + 1, nyb - 1)], right[b])
                y_down = jnp.where(lane == 0, left[max(b - 1, 0)], left[b])
                x_up = jnp.where(
                    sub == across - 1,
                    from_hi[t, pl.ds(b * layers + k, 1), :],
                    pltpu.roll(here, across - 1, 0),
                )
                x_down = jnp.where(
                    sub == 0, from_lo[t, pl.ds(b * layers + k, 1), :], pltpu.roll(here, 1, 0)
                )
                z_up = fields[t, pl.ds(base + 2 * slab + b * across, across), :]
                z_down = fields[t, own, :]
                new = (
                    (c0[own, :] * here + gyp[own, :] * y_up)
                    + (gym[own, :] * y_down + gxp[own, :] * (x_up - here))
                ) + (
                    (gxm[own, :] * (x_down - here)
                     + gz[pl.ds(base + slab + b * across, across), :] * z_up)
                    + (gz[own, :] * z_down + mis[t, own, :])
                )
                if last:
                    adjoint[own, :] = new
                    acc = new
                    for s in range(1, steps):
                        acc = acc + fields[s, pl.ds(base + slab + b * across, across), :]
                    total[pl.ds(base + b, across, stride=nyb), :] = acc
                else:
                    fields[t + 1, pl.ds(base + slab + b * across, across), :] = new
            return 0

        lax.fori_loop(0, layers, body, 0)

    for t in range(steps):
        last = t == steps - 1
        loads[t].wait()
        if t > 0:
            receive(t)
        if not last:
            edges(t)
            send(t + 1)
        interior(t, last)

    load_prof.wait()

    unroll = 32

    def pick(c, _):
        base = pl.multiple_of(c * unroll, unroll)
        for j in range(unroll):
            picked[pl.ds(base + j, 1), :] = total[pl.ds(block[base + j], 1), :]
        return 0

    lax.fori_loop(0, entries // unroll, pick, 0)

    chunk = 512
    sums = jnp.zeros((n * pad_rows, 3 * LANES), jnp.float32)
    for c in range(entries // chunk):
        own = pl.ds(c * chunk, chunk)
        value = DT * jnp.sum(
            picked[own, :] * prof[own, :], axis=1, keepdims=True
        )
        spread = one_lo[own, :] * value
        first = spread.astype(jnp.bfloat16)
        rest = spread - first.astype(jnp.float32)
        second = rest.astype(jnp.bfloat16)
        third = (rest - second.astype(jnp.float32)).astype(jnp.bfloat16)
        sums = sums + jnp.dot(
            one_hi[:, c * chunk : (c + 1) * chunk],
            jnp.concatenate([first, second, third], axis=1),
            preferred_element_type=jnp.float32,
        )
    dense[...] = (
        (sums[:, 2 * LANES :] + sums[:, LANES : 2 * LANES]) + sums[:, :LANES]
    ).reshape(n, pad_rows, LANES)

    def deliver(d):
        peer = lax.rem(me + d, n)
        return pltpu.make_async_remote_copy(
            src_ref=dense.at[peer],
            dst_ref=parts.at[d],
            send_sem=out_sems.at[d],
            recv_sem=in_sems.at[d],
            device_id={"gx": peer},
            device_id_type=MESH,
        )

    def start(d, _):
        deliver(d).start()
        return 0

    lax.fori_loop(1, n, start, 0)

    for t in range(steps):
        @pl.when(me < n - 1)
        def _():
            hop(t, True).wait_send()

        @pl.when(me > 0)
        def _():
            hop(t, False).wait_send()

    def finish(d, acc):
        deliver(d).wait_recv()
        return acc + parts[d]

    result = lax.fori_loop(1, n, finish, dense[me])
    grad[...] = result[:owner_rows]

    def drain(d, _):
        deliver(d).wait_send()
        return 0

    lax.fori_loop(1, n, drain, 0)


def on_device(
    terminal, misfit, material, material_table, heater_slot, entry_heater, entry_block, profile
):
    n = lax.axis_size("gx")
    layers, across, depth = terminal.shape
    steps = misfit.shape[0]
    mats = material_table.shape[1]
    nyb = depth // LANES
    entries = entry_block.shape[0]
    per_owner = heater_slot.shape[0] // n
    rows, slab, edge = layers * across * nyb, across * nyb, layers * nyb
    pad_rows = ceil8(per_owner // LANES)
    term = terminal.reshape(layers, across, nyb, LANES).swapaxes(1, 2).reshape(rows, LANES)
    mis = (
        misfit.reshape(steps, layers, across, nyb, LANES).swapaxes(2, 3).reshape(steps, rows, LANES)
    )
    hbm = pl.BlockSpec(memory_space=pltpu.HBM)
    vmem = pl.BlockSpec(memory_space=pltpu.VMEM)
    f32 = jnp.float32
    adjoint, grad = pl.pallas_call(
        functools.partial(kernel, n, layers, across, nyb, steps, mats, per_owner),
        out_shape=(
            jax.ShapeDtypeStruct((rows, LANES), f32),
            jax.ShapeDtypeStruct((per_owner // LANES, LANES), f32),
        ),
        in_specs=[hbm] * 8,
        out_specs=(vmem, vmem),
        scratch_shapes=[
            pltpu.VMEM((layers * across, nyb), jnp.int32),
            pltpu.SMEM(material_table.shape, f32),
            pltpu.VMEM((heater_slot.shape[0] // LANES, LANES), jnp.int32),
            pltpu.VMEM((entries // LANES, LANES), jnp.int32),
            pltpu.SMEM((entries,), jnp.int32),
            pltpu.VMEM((steps, rows + 2 * slab, LANES), f32),
            pltpu.VMEM((steps, rows, LANES), f32),
            pltpu.VMEM((entries, LANES), f32),
            pltpu.VMEM((rows, LANES), f32),
            pltpu.VMEM((rows, LANES), f32),
            pltpu.VMEM((rows, LANES), f32),
            pltpu.VMEM((rows, LANES), f32),
            pltpu.VMEM((rows + slab, LANES), f32),
            pltpu.VMEM((rows, LANES), f32),
            pltpu.VMEM((layers * across, LANES), f32),
            pltpu.VMEM((layers * across, LANES), f32),
            pltpu.VMEM((rows, LANES), f32),
            pltpu.VMEM((entries, LANES), f32),
            pltpu.VMEM((entries, LANES), f32),
            pltpu.VMEM((n * pad_rows, entries), jnp.bfloat16),
            pltpu.VMEM((n, pad_rows, LANES), f32),
            pltpu.VMEM((steps, edge + layers, LANES), f32),
            pltpu.VMEM((steps, edge + layers, LANES), f32),
            pltpu.VMEM((steps, edge + layers, LANES), f32),
            pltpu.VMEM((steps, edge + layers, LANES), f32),
            pltpu.VMEM((n, pad_rows, LANES), f32),
            pltpu.SemaphoreType.DMA,
            pltpu.SemaphoreType.DMA((steps,)),
            pltpu.SemaphoreType.DMA,
            pltpu.SemaphoreType.DMA((5,)),
            pltpu.SemaphoreType.DMA((steps, 2)),
            pltpu.SemaphoreType.DMA((steps, 2)),
            pltpu.SemaphoreType.DMA((n,)),
            pltpu.SemaphoreType.DMA((n,)),
        ],
        compiler_params=pltpu.CompilerParams(
            collective_id=0, has_side_effects=True, vmem_limit_bytes=48 * 1024 * 1024
        ),
    )(
        term,
        mis,
        material.reshape(layers * across, nyb),
        material_table,
        heater_slot.reshape(-1, LANES),
        entry_heater.reshape(-1, LANES),
        entry_block,
        profile,
    )
    adjoint = adjoint.reshape(layers, nyb, across, LANES).swapaxes(1, 2).reshape(terminal.shape)
    return (adjoint, grad.reshape(per_owner))


def solution(mesh):
    return jax.shard_map(
        on_device,
        mesh=mesh,
        in_specs=(
            P("groups", "gx", None),
            P(None, "groups", "gx", None),
            P(None, "gx", None),
            P(),
            P(),
            P("gx"),
            P("gx"),
            P("gx", None),
        ),
        out_specs=(P("groups", "gx", None), P(("groups", "gx"))),
        check_vma=False,
    )
```

```python
import functools

import jax
import jax.numpy as jnp
from jax import lax
from jax.experimental import pallas as pl
from jax.experimental.pallas import tpu as pltpu
from jax.sharding import PartitionSpec as P

MESH = pl.DeviceIdType.MESH
DT = 0.16
LANES = 128


def ceil8(rows):
    return (rows + 7) // 8 * 8


def kernel(
    n, layers, across, nyb, steps, mats, per_owner,
    term, misfit, mat_hbm, table_hbm, slots_hbm, heaters_hbm, block_hbm, profile,
    adjoint, grad,
    mat, table, slot_table, heaters, block,
    fields, mis, prof, gxp, gxm, gyp, gym, gz, c0, rim, packed, vpacked, total, picked,
    one_lo, one_hi, dense, send_lo, send_hi, from_lo, from_hi, parts,
    sem_term, sem_mis, sem_prof, sem_small, send_sems, recv_sems, out_sems, in_sems,
):
    me = lax.axis_index("gx")
    slab = nyb * across
    rows = layers * slab
    edge = nyb * layers
    table_rows = slot_table.shape[0]
    entries = heaters.shape[0] * LANES
    owner_rows = per_owner // LANES
    pad_rows = ceil8(owner_rows)

    barrier = pltpu.get_barrier_semaphore()

    def greet(d, _):
        pl.semaphore_signal(
            barrier, inc=1, device_id={"gx": lax.rem(me + d, n)}, device_id_type=MESH
        )
        return 0

    lax.fori_loop(1, n, greet, 0)

    small = [
        pltpu.make_async_copy(source, target, sem_small.at[i])
        for i, (source, target) in enumerate((
            (mat_hbm, mat), (table_hbm, table), (slots_hbm, slot_table),
            (heaters_hbm, heaters), (block_hbm, block),
        ))
    ]
    for load in small:
        load.start()
    load_term = pltpu.make_async_copy(term, fields.at[0, pl.ds(slab, rows)], sem_term)
    load_term.start()
    loads = [
        pltpu.make_async_copy(misfit.at[t], mis.at[t], sem_mis.at[t]) for t in range(steps)
    ]
    for load in loads:
        load.start()
    load_prof = pltpu.make_async_copy(profile, prof, sem_prof)
    load_prof.start()

    sub = lax.broadcasted_iota(jnp.int32, (across, LANES), 0)
    lane = lax.broadcasted_iota(jnp.int32, (across, LANES), 1)
    lane_e = lax.broadcasted_iota(jnp.int32, (layers, LANES), 1)

    small[0].wait()
    small[1].wait()
    index = mat[...]
    lat = jnp.zeros(index.shape, jnp.float32)
    ver = jnp.zeros(index.shape, jnp.float32)
    for m in range(mats):
        lat = jnp.where(index == m, table[0, m], lat)
        ver = jnp.where(index == m, table[1, m], ver)
    packed[...] = jnp.zeros(packed.shape, jnp.float32)
    vpacked[...] = jnp.zeros(vpacked.shape, jnp.float32)
    packed[:, pl.ds(0, nyb)] = lat
    vpacked[:, pl.ds(0, nyb)] = ver

    zeros_slab = jnp.zeros((slab, LANES), jnp.float32)
    for t in range(steps):
        fields[t, pl.ds(0, slab), :] = zeros_slab
        fields[t, pl.ds(slab + rows, slab), :] = zeros_slab
    gz[pl.ds(0, slab), :] = zeros_slab
    gz[pl.ds(rows, slab), :] = zeros_slab

    @pl.when(me == 0)
    def _():
        from_lo[...] = jnp.zeros(from_lo.shape, jnp.float32)

    @pl.when(me == n - 1)
    def _():
        from_hi[...] = jnp.zeros(from_hi.shape, jnp.float32)

    def hop(t, up):
        count = edge + layers if t == 0 else edge
        s = 1 if up else 0
        return pltpu.make_async_remote_copy(
            src_ref=(send_hi if up else send_lo).at[t, pl.ds(0, count)],
            dst_ref=(from_lo if up else from_hi).at[t, pl.ds(0, count)],
            send_sem=send_sems.at[t, s],
            recv_sem=recv_sems.at[t, s],
            device_id={"gx": me + 1 if up else me - 1},
            device_id_type=MESH,
        )

    def send(t):
        @pl.when(me < n - 1)
        def _():
            hop(t, True).start()

        @pl.when(me > 0)
        def _():
            hop(t, False).start()

    def receive(t):
        @pl.when(me > 0)
        def _():
            hop(t, True).wait_recv()

        @pl.when(me < n - 1)
        def _():
            hop(t, False).wait_recv()

    load_term.wait()
    for s, (buffer, x) in enumerate(((send_lo, 0), (send_hi, across - 1))):
        for b in range(nyb):
            buffer[0, pl.ds(b * layers, layers), :] = fields[
                0, pl.ds(slab + b * across + x, layers, stride=slab), :
            ]
        buffer[0, pl.ds(edge, layers), :] = packed[pl.ds(x, layers, stride=across), :]
    pl.semaphore_wait(barrier, n - 1)
    send(0)

    half = 0.5 * DT

    def coefficients(k, _):
        at = pl.multiple_of(k * across, across)
        base = pl.multiple_of(k * slab, slab)
        lat = packed[pl.ds(at, across), :]
        ver = vpacked[pl.ds(at, across), :]
        upper = jnp.minimum(k + 1, layers - 1)
        ver_up = vpacked[pl.ds(pl.multiple_of(upper * across, across), across), :]
        lower = jnp.maximum(k - 1, 0)
        ver_down = vpacked[pl.ds(pl.multiple_of(lower * across, across), across), :]
        z_up = jnp.where(k < layers - 1, half, 0.0) * (ver + ver_up)
        z_down = jnp.where(k > 0, half, 0.0) * (ver + ver_down)
        x_up = half * (lat + pltpu.roll(lat, across - 1, 0))
        x_down = half * (lat + pltpu.roll(lat, 1, 0))
        side = half * (lat + pltpu.roll(lat, LANES - 1, 1))
        inner = DT * lat
        center = 1.0 - z_up - z_down

        def wide(value, b):
            return jnp.broadcast_to(value[:, b : b + 1], (across, LANES))

        none = jnp.zeros((across, LANES), jnp.float32)
        sides = [none] + [wide(side, b) for b in range(nyb - 1)] + [none]
        for b in range(nyb):
            own = pl.ds(base + b * across, across)
            y = wide(inner, b)
            y_up = jnp.where(lane == LANES - 1, sides[b + 1], y)
            y_down = jnp.where(lane == 0, sides[b], y)
            gyp[own, :] = y_up
            gym[own, :] = y_down
            gxp[own, :] = wide(x_up, b)
            gxm[own, :] = wide(x_down, b)
            gz[pl.ds(base + slab + b * across, across), :] = wide(z_up, b)
            c0[own, :] = wide(center, b) - y_up - y_down
        return 0

    lax.fori_loop(0, layers, coefficients, 0)

    row_e = lax.broadcasted_iota(jnp.int32, (layers, LANES), 0)
    for s, x, inward in ((0, 0, 1), (1, across - 1, -1)):
        lat = packed[pl.ds(x, layers, stride=across), :]
        ver = vpacked[pl.ds(x, layers, stride=across), :]
        g_in = half * (lat + packed[pl.ds(x + inward, layers, stride=across), :])
        z_up = jnp.where(row_e < layers - 1, half * (ver + pltpu.roll(ver, layers - 1, 0)), 0.0)
        z_down = jnp.where(row_e > 0, half * (ver + pltpu.roll(ver, 1, 0)), 0.0)
        side = half * (lat + pltpu.roll(lat, LANES - 1, 1))
        inner = DT * lat
        center = 1.0 - z_up - z_down - g_in

        def wide_e(value, b):
            return jnp.broadcast_to(value[:, b : b + 1], (layers, LANES))

        none = jnp.zeros((layers, LANES), jnp.float32)
        sides = [none] + [wide_e(side, b) for b in range(nyb - 1)] + [none]
        for b in range(nyb):
            own = pl.ds(b * layers, layers)
            y = wide_e(inner, b)
            y_up = jnp.where(lane_e == LANES - 1, sides[b + 1], y)
            y_down = jnp.where(lane_e == 0, sides[b], y)
            rim[s, 0, own, :] = wide_e(center, b) - y_up - y_down
            rim[s, 1, own, :] = y_up
            rim[s, 2, own, :] = y_down
            rim[s, 3, own, :] = wide_e(g_in, b)
            rim[s, 4, own, :] = wide_e(z_up, b)
            rim[s, 5, own, :] = wide_e(z_down, b)

    for load in small[2:]:
        load.wait()
    cut = 4
    width = cut * LANES
    slots = slot_table[...]
    pieces = jnp.concatenate(
        [
            jnp.right_shift(slots, 8).astype(jnp.float32).T,
            jnp.bitwise_and(slots, 255).astype(jnp.float32).T,
        ],
        axis=0,
    ).astype(jnp.bfloat16)

    def lookup(c, _):
        heater = jnp.concatenate(
            [heaters[pl.ds(c * cut + j, 1), :] for j in range(cut)], axis=1
        )
        high = (
            lax.broadcasted_iota(jnp.int32, (table_rows, width), 0)
            == jnp.right_shift(heater, 7)
        ).astype(jnp.float32).astype(jnp.bfloat16)
        found = jnp.dot(pieces, high, preferred_element_type=jnp.float32)
        lanes = lax.broadcasted_iota(jnp.int32, (LANES, width), 0)
        mine = lanes == jnp.bitwise_and(heater, LANES - 1)
        big = jnp.sum(jnp.where(mine, found[:LANES], 0.0), axis=0, keepdims=True)
        small = jnp.sum(jnp.where(mine, found[LANES:], 0.0), axis=0, keepdims=True)
        slot = (big * 256.0 + small).astype(jnp.int32)
        owner = slot // per_owner
        place = owner * pad_rows + (slot - owner * per_owner) // LANES
        one_hi[:, pl.ds(pl.multiple_of(c * width, width), width)] = (
            lax.broadcasted_iota(jnp.int32, (n * pad_rows, width), 0) == place
        ).astype(jnp.float32).astype(jnp.bfloat16)
        low = (lanes == jnp.bitwise_and(slot, LANES - 1)).astype(jnp.float32)
        for j in range(cut):
            one_lo[pl.ds(pl.multiple_of(c * width, width) + j * LANES, LANES), :] = low[
                :, j * LANES : (j + 1) * LANES
            ].T
        return 0

    lookups = entries // width
    lax.fori_loop(0, lookups, lookup, 0)

    def edges_ready(t):
        for s, x, inward, buffer in ((0, 0, 1, send_lo), (1, across - 1, -1, send_hi)):
            v = [buffer[t, pl.ds(b * layers, layers), :] for b in range(nyb)]
            right = [pltpu.roll(u, LANES - 1, 1) for u in v]
            left = [pltpu.roll(u, 1, 1) for u in v]
            for b in range(nyb):
                own = pl.ds(b * layers, layers)
                y_up = jnp.where(lane_e == LANES - 1, right[min(b + 1, nyb - 1)], right[b])
                y_down = jnp.where(lane_e == 0, left[max(b - 1, 0)], left[b])
                inner = fields[t, pl.ds(slab + b * across + x + inward, layers, stride=slab), :]
                buffer[t + 1, own, :] = (
                    (rim[s, 0, own, :] * v[b] + rim[s, 1, own, :] * y_up)
                    + (rim[s, 2, own, :] * y_down + rim[s, 3, own, :] * inner)
                ) + (
                    (rim[s, 4, own, :] * pltpu.roll(v[b], layers - 1, 0)
                     + rim[s, 5, own, :] * pltpu.roll(v[b], 1, 0))
                    + mis[t, pl.ds(b * across + x, layers, stride=slab), :]
                )

    def edges_done(t):
        whole = pl.ds(0, edge)
        for s, arrived, buffer in ((0, from_lo, send_lo), (1, from_hi, send_hi)):
            buffer[t + 1, whole, :] = buffer[t + 1, whole, :] + rim[s, 6, :, :] * (
                arrived[t, whole, :] - buffer[t, whole, :]
            )

    def interior(t, last):
        def body(k, _):
            base = pl.multiple_of(k * slab, slab)
            v = [fields[t, pl.ds(base + slab + b * across, across), :] for b in range(nyb)]
            right = [pltpu.roll(u, LANES - 1, 1) for u in v]
            left = [pltpu.roll(u, 1, 1) for u in v]
            for b in range(nyb):
                own = pl.ds(base + b * across, across)
                here = v[b]
                y_up = jnp.where(lane == LANES - 1, right[min(b + 1, nyb - 1)], right[b])
                y_down = jnp.where(lane == 0, left[max(b - 1, 0)], left[b])
                x_up = jnp.where(
                    sub == across - 1,
                    from_hi[t, pl.ds(b * layers + k, 1), :],
                    pltpu.roll(here, across - 1, 0),
                )
                x_down = jnp.where(
                    sub == 0, from_lo[t, pl.ds(b * layers + k, 1), :], pltpu.roll(here, 1, 0)
                )
                z_up = fields[t, pl.ds(base + 2 * slab + b * across, across), :]
                z_down = fields[t, own, :]
                new = (
                    (c0[own, :] * here + gyp[own, :] * y_up)
                    + (gym[own, :] * y_down + gxp[own, :] * (x_up - here))
                ) + (
                    (gxm[own, :] * (x_down - here)
                     + gz[pl.ds(base + slab + b * across, across), :] * z_up)
                    + (gz[own, :] * z_down + mis[t, own, :])
                )
                if last:
                    adjoint[own, :] = new
                    acc = new
                    for s in range(1, steps):
                        acc = acc + fields[s, pl.ds(base + slab + b * across, across), :]
                    total[pl.ds(base + b, across, stride=nyb), :] = acc
                else:
                    fields[t + 1, pl.ds(base + slab + b * across, across), :] = new
            return 0

        lax.fori_loop(0, layers, body, 0)

    loads[0].wait()
    edges_ready(0)
    receive(0)
    for s, x, ref, arrived, outside in (
        (0, 0, gxm, from_lo, me == 0),
        (1, across - 1, gxp, from_hi, me == n - 1),
    ):
        scale = jnp.where(outside, 0.0, half)
        pair = scale * (
            packed[pl.ds(x, layers, stride=across), :] + arrived[0, pl.ds(edge, layers), :]
        )
        for b in range(nyb):
            value = jnp.broadcast_to(pair[:, b : b + 1], (layers, LANES))
            ref[pl.ds(b * across + x, layers, stride=slab), :] = value
            rim[s, 6, pl.ds(b * layers, layers), :] = value

    for t in range(steps):
        last = t == steps - 1
        if t > 0:
            loads[t].wait()
            if not last:
                edges_ready(t)
            receive(t)
        if not last:
            edges_done(t)
            send(t + 1)
        interior(t, last)

    load_prof.wait()

    unroll = 32

    def pick(c, _):
        base = pl.multiple_of(c * unroll, unroll)
        for j in range(unroll):
            picked[pl.ds(base + j, 1), :] = total[pl.ds(block[base + j], 1), :]
        return 0

    lax.fori_loop(0, entries // unroll, pick, 0)

    chunk = 512
    sums = jnp.zeros((n * pad_rows, 3 * LANES), jnp.float32)
    for c in range(entries // chunk):
        own = pl.ds(c * chunk, chunk)
        value = DT * jnp.sum(
            picked[own, :] * prof[own, :], axis=1, keepdims=True
        )
        spread = one_lo[own, :] * value
        first = spread.astype(jnp.bfloat16)
        rest = spread - first.astype(jnp.float32)
        second = rest.astype(jnp.bfloat16)
        third = (rest - second.astype(jnp.float32)).astype(jnp.bfloat16)
        sums = sums + jnp.dot(
            one_hi[:, c * chunk : (c + 1) * chunk],
            jnp.concatenate([first, second, third], axis=1),
            preferred_element_type=jnp.float32,
        )
    dense[...] = (
        (sums[:, 2 * LANES :] + sums[:, LANES : 2 * LANES]) + sums[:, :LANES]
    ).reshape(n, pad_rows, LANES)

    def deliver(d):
        peer = lax.rem(me + d, n)
        return pltpu.make_async_remote_copy(
            src_ref=dense.at[peer],
            dst_ref=parts.at[d],
            send_sem=out_sems.at[d],
            recv_sem=in_sems.at[d],
            device_id={"gx": peer},
            device_id_type=MESH,
        )

    def start(d, _):
        deliver(d).start()
        return 0

    lax.fori_loop(1, n, start, 0)

    for t in range(steps):
        @pl.when(me < n - 1)
        def _():
            hop(t, True).wait_send()

        @pl.when(me > 0)
        def _():
            hop(t, False).wait_send()

    def finish(d, acc):
        deliver(d).wait_recv()
        return acc + parts[d]

    result = lax.fori_loop(1, n, finish, dense[me])
    grad[...] = result[:owner_rows]

    def drain(d, _):
        deliver(d).wait_send()
        return 0

    lax.fori_loop(1, n, drain, 0)


def on_device(
    terminal, misfit, material, material_table, heater_slot, entry_heater, entry_block, profile
):
    n = lax.axis_size("gx")
    layers, across, depth = terminal.shape
    steps = misfit.shape[0]
    mats = material_table.shape[1]
    nyb = depth // LANES
    entries = entry_block.shape[0]
    per_owner = heater_slot.shape[0] // n
    rows, slab, edge = layers * across * nyb, across * nyb, layers * nyb
    pad_rows = ceil8(per_owner // LANES)
    term = terminal.reshape(layers, across, nyb, LANES).swapaxes(1, 2).reshape(rows, LANES)
    mis = (
        misfit.reshape(steps, layers, across, nyb, LANES).swapaxes(2, 3).reshape(steps, rows, LANES)
    )
    hbm = pl.BlockSpec(memory_space=pltpu.HBM)
    vmem = pl.BlockSpec(memory_space=pltpu.VMEM)
    f32 = jnp.float32
    adjoint, grad = pl.pallas_call(
        functools.partial(kernel, n, layers, across, nyb, steps, mats, per_owner),
        out_shape=(
            jax.ShapeDtypeStruct((rows, LANES), f32),
            jax.ShapeDtypeStruct((per_owner // LANES, LANES), f32),
        ),
        in_specs=[hbm] * 8,
        out_specs=(vmem, vmem),
        scratch_shapes=[
            pltpu.VMEM((layers * across, nyb), jnp.int32),
            pltpu.SMEM(material_table.shape, f32),
            pltpu.VMEM((heater_slot.shape[0] // LANES, LANES), jnp.int32),
            pltpu.VMEM((entries // LANES, LANES), jnp.int32),
            pltpu.SMEM((entries,), jnp.int32),
            pltpu.VMEM((steps, rows + 2 * slab, LANES), f32),
            pltpu.VMEM((steps, rows, LANES), f32),
            pltpu.VMEM((entries, LANES), f32),
            pltpu.VMEM((rows, LANES), f32),
            pltpu.VMEM((rows, LANES), f32),
            pltpu.VMEM((rows, LANES), f32),
            pltpu.VMEM((rows, LANES), f32),
            pltpu.VMEM((rows + slab, LANES), f32),
            pltpu.VMEM((rows, LANES), f32),
            pltpu.VMEM((2, 7, edge, LANES), f32),
            pltpu.VMEM((layers * across, LANES), f32),
            pltpu.VMEM((layers * across, LANES), f32),
            pltpu.VMEM((rows, LANES), f32),
            pltpu.VMEM((entries, LANES), f32),
            pltpu.VMEM((entries, LANES), f32),
            pltpu.VMEM((n * pad_rows, entries), jnp.bfloat16),
            pltpu.VMEM((n, pad_rows, LANES), f32),
            pltpu.VMEM((steps, edge + layers, LANES), f32),
            pltpu.VMEM((steps, edge + layers, LANES), f32),
            pltpu.VMEM((steps, edge + layers, LANES), f32),
            pltpu.VMEM((steps, edge + layers, LANES), f32),
            pltpu.VMEM((n, pad_rows, LANES), f32),
            pltpu.SemaphoreType.DMA,
            pltpu.SemaphoreType.DMA((steps,)),
            pltpu.SemaphoreType.DMA,
            pltpu.SemaphoreType.DMA((5,)),
            pltpu.SemaphoreType.DMA((steps, 2)),
            pltpu.SemaphoreType.DMA((steps, 2)),
            pltpu.SemaphoreType.DMA((n,)),
            pltpu.SemaphoreType.DMA((n,)),
        ],
        compiler_params=pltpu.CompilerParams(
            collective_id=0, has_side_effects=True, vmem_limit_bytes=64 * 1024 * 1024
        ),
    )(
        term,
        mis,
        material.reshape(layers * across, nyb),
        material_table,
        heater_slot.reshape(-1, LANES),
        entry_heater.reshape(-1, LANES),
        entry_block,
        profile,
    )
    adjoint = adjoint.reshape(layers, nyb, across, LANES).swapaxes(1, 2).reshape(terminal.shape)
    return (adjoint, grad.reshape(per_owner))


def solution(mesh):
    return jax.shard_map(
        on_device,
        mesh=mesh,
        in_specs=(
            P("groups", "gx", None),
            P(None, "groups", "gx", None),
            P(None, "gx", None),
            P(),
            P(),
            P("gx"),
            P("gx"),
            P("gx", None),
        ),
        out_specs=(P("groups", "gx", None), P(("groups", "gx"))),
        check_vma=False,
    )
```

```python
import functools

import jax
import jax.numpy as jnp
from jax import lax
from jax.experimental import pallas as pl
from jax.experimental.pallas import tpu as pltpu
from jax.sharding import PartitionSpec as P

MESH = pl.DeviceIdType.MESH
DT = 0.16
LANES = 128


def ceil8(rows):
    return (rows + 7) // 8 * 8


def kernel(
    n, layers, across, nyb, steps, mats, per_owner,
    term, misfit, mat_hbm, table_hbm, slots_hbm, heaters_hbm, block_hbm, profile,
    adjoint, grad,
    mat, table, slot_table, heaters, block,
    fields, mis, prof, gxp, gxm, gyp, gym, gz, c0, rim, packed, vpacked, total, picked, final,
    one_lo, one_hi, dense, send_lo, send_hi, from_lo, from_hi, parts,
    sem_term, sem_mis, sem_prof, sem_small, send_sems, recv_sems, out_sems, in_sems, sem_out,
):
    me = lax.axis_index("gx")
    slab = nyb * across
    rows = layers * slab
    edge = nyb * layers
    table_rows = slot_table.shape[0]
    entries = heaters.shape[0] * LANES
    owner_rows = per_owner // LANES
    pad_rows = ceil8(owner_rows)

    barrier = pltpu.get_barrier_semaphore()

    def greet(d, _):
        pl.semaphore_signal(
            barrier, inc=1, device_id={"gx": lax.rem(me + d, n)}, device_id_type=MESH
        )
        return 0

    lax.fori_loop(1, n, greet, 0, unroll=n <= 16)

    small = [
        pltpu.make_async_copy(source, target, sem_small.at[i])
        for i, (source, target) in enumerate((
            (mat_hbm, mat), (table_hbm, table), (slots_hbm, slot_table),
            (heaters_hbm, heaters), (block_hbm, block),
        ))
    ]
    for load in small:
        load.start()
    load_term = pltpu.make_async_copy(term, fields.at[0, pl.ds(slab, rows)], sem_term)
    load_term.start()
    loads = [
        pltpu.make_async_copy(misfit.at[t], mis.at[t], sem_mis.at[t]) for t in range(steps)
    ]
    for load in loads:
        load.start()
    load_prof = pltpu.make_async_copy(profile, prof, sem_prof)
    load_prof.start()

    sub = lax.broadcasted_iota(jnp.int32, (across, LANES), 0)
    lane = lax.broadcasted_iota(jnp.int32, (across, LANES), 1)
    lane_e = lax.broadcasted_iota(jnp.int32, (layers, LANES), 1)

    small[0].wait()
    small[1].wait()
    index = mat[...]
    lat = jnp.zeros(index.shape, jnp.float32)
    ver = jnp.zeros(index.shape, jnp.float32)
    for m in range(mats):
        lat = jnp.where(index == m, table[0, m], lat)
        ver = jnp.where(index == m, table[1, m], ver)
    packed[...] = jnp.zeros(packed.shape, jnp.float32)
    vpacked[...] = jnp.zeros(vpacked.shape, jnp.float32)
    packed[:, pl.ds(0, nyb)] = lat
    vpacked[:, pl.ds(0, nyb)] = ver

    zeros_slab = jnp.zeros((slab, LANES), jnp.float32)
    for t in range(steps):
        fields[t, pl.ds(0, slab), :] = zeros_slab
        fields[t, pl.ds(slab + rows, slab), :] = zeros_slab
    gz[pl.ds(0, slab), :] = zeros_slab
    gz[pl.ds(rows, slab), :] = zeros_slab

    @pl.when(me == 0)
    def _():
        from_lo[...] = jnp.zeros(from_lo.shape, jnp.float32)

    @pl.when(me == n - 1)
    def _():
        from_hi[...] = jnp.zeros(from_hi.shape, jnp.float32)

    def hop(t, up):
        count = edge + layers if t == 0 else edge
        s = 1 if up else 0
        return pltpu.make_async_remote_copy(
            src_ref=(send_hi if up else send_lo).at[t, pl.ds(0, count)],
            dst_ref=(from_lo if up else from_hi).at[t, pl.ds(0, count)],
            send_sem=send_sems.at[t, s],
            recv_sem=recv_sems.at[t, s],
            device_id={"gx": me + 1 if up else me - 1},
            device_id_type=MESH,
        )

    def send(t):
        @pl.when(me < n - 1)
        def _():
            hop(t, True).start()

        @pl.when(me > 0)
        def _():
            hop(t, False).start()

    def receive(t):
        @pl.when(me > 0)
        def _():
            hop(t, True).wait_recv()

        @pl.when(me < n - 1)
        def _():
            hop(t, False).wait_recv()

    load_term.wait()
    for s, (buffer, x) in enumerate(((send_lo, 0), (send_hi, across - 1))):
        for b in range(nyb):
            buffer[0, pl.ds(b * layers, layers), :] = fields[
                0, pl.ds(slab + b * across + x, layers, stride=slab), :
            ]
        buffer[0, pl.ds(edge, layers), :] = packed[pl.ds(x, layers, stride=across), :]

    pl.semaphore_wait(barrier, n - 1)
    send(0)

    half = 0.5 * DT

    def coefficients(k, _):
        at = pl.multiple_of(k * across, across)
        base = pl.multiple_of(k * slab, slab)
        lat = packed[pl.ds(at, across), :]
        ver = vpacked[pl.ds(at, across), :]
        upper = jnp.minimum(k + 1, layers - 1)
        ver_up = vpacked[pl.ds(pl.multiple_of(upper * across, across), across), :]
        lower = jnp.maximum(k - 1, 0)
        ver_down = vpacked[pl.ds(pl.multiple_of(lower * across, across), across), :]
        z_up = jnp.where(k < layers - 1, half, 0.0) * (ver + ver_up)
        z_down = jnp.where(k > 0, half, 0.0) * (ver + ver_down)
        x_up = half * (lat + pltpu.roll(lat, across - 1, 0))
        x_down = half * (lat + pltpu.roll(lat, 1, 0))
        side = half * (lat + pltpu.roll(lat, LANES - 1, 1))
        inner = DT * lat
        center = 1.0 - z_up - z_down

        def wide(value, b):
            return jnp.broadcast_to(value[:, b : b + 1], (across, LANES))

        none = jnp.zeros((across, LANES), jnp.float32)
        sides = [none] + [wide(side, b) for b in range(nyb - 1)] + [none]
        for b in range(nyb):
            own = pl.ds(base + b * across, across)
            y = wide(inner, b)
            y_up = jnp.where(lane == LANES - 1, sides[b + 1], y)
            y_down = jnp.where(lane == 0, sides[b], y)
            gyp[own, :] = y_up
            gym[own, :] = y_down
            gxp[own, :] = wide(x_up, b)
            gxm[own, :] = wide(x_down, b)
            gz[pl.ds(base + slab + b * across, across), :] = wide(z_up, b)
            c0[own, :] = wide(center, b) - y_up - y_down
        return 0

    lax.fori_loop(0, layers, coefficients, 0)

    row_e = lax.broadcasted_iota(jnp.int32, (layers, LANES), 0)
    for s, x, inward in ((0, 0, 1), (1, across - 1, -1)):
        lat = packed[pl.ds(x, layers, stride=across), :]
        ver = vpacked[pl.ds(x, layers, stride=across), :]
        g_in = half * (lat + packed[pl.ds(x + inward, layers, stride=across), :])
        z_up = jnp.where(row_e < layers - 1, half * (ver + pltpu.roll(ver, layers - 1, 0)), 0.0)
        z_down = jnp.where(row_e > 0, half * (ver + pltpu.roll(ver, 1, 0)), 0.0)
        side = half * (lat + pltpu.roll(lat, LANES - 1, 1))
        inner = DT * lat
        center = 1.0 - z_up - z_down - g_in

        def wide_e(value, b):
            return jnp.broadcast_to(value[:, b : b + 1], (layers, LANES))

        none = jnp.zeros((layers, LANES), jnp.float32)
        sides = [none] + [wide_e(side, b) for b in range(nyb - 1)] + [none]
        for b in range(nyb):
            own = pl.ds(b * layers, layers)
            y = wide_e(inner, b)
            y_up = jnp.where(lane_e == LANES - 1, sides[b + 1], y)
            y_down = jnp.where(lane_e == 0, sides[b], y)
            rim[s, 0, own, :] = wide_e(center, b) - y_up - y_down
            rim[s, 1, own, :] = y_up
            rim[s, 2, own, :] = y_down
            rim[s, 3, own, :] = wide_e(g_in, b)
            rim[s, 4, own, :] = wide_e(z_up, b)
            rim[s, 5, own, :] = wide_e(z_down, b)

    for load in small[2:]:
        load.wait()
    cut = 4
    width = cut * LANES
    slots = slot_table[...]
    pieces = jnp.concatenate(
        [
            jnp.right_shift(slots, 8).astype(jnp.float32).T,
            jnp.bitwise_and(slots, 255).astype(jnp.float32).T,
        ],
        axis=0,
    ).astype(jnp.bfloat16)

    def lookup(c, _):
        heater = jnp.concatenate(
            [heaters[pl.ds(c * cut + j, 1), :] for j in range(cut)], axis=1
        )
        high = (
            lax.broadcasted_iota(jnp.int32, (table_rows, width), 0)
            == jnp.right_shift(heater, 7)
        ).astype(jnp.float32).astype(jnp.bfloat16)
        found = jnp.dot(pieces, high, preferred_element_type=jnp.float32)
        lanes = lax.broadcasted_iota(jnp.int32, (LANES, width), 0)
        mine = lanes == jnp.bitwise_and(heater, LANES - 1)
        big = jnp.sum(jnp.where(mine, found[:LANES], 0.0), axis=0, keepdims=True)
        small = jnp.sum(jnp.where(mine, found[LANES:], 0.0), axis=0, keepdims=True)
        slot = (big * 256.0 + small).astype(jnp.int32)
        owner = slot // per_owner
        place = owner * pad_rows + (slot - owner * per_owner) // LANES
        one_hi[:, pl.ds(pl.multiple_of(c * width, width), width)] = (
            lax.broadcasted_iota(jnp.int32, (n * pad_rows, width), 0) == place
        ).astype(jnp.float32).astype(jnp.bfloat16)
        low = (lanes == jnp.bitwise_and(slot, LANES - 1)).astype(jnp.float32)
        for j in range(cut):
            one_lo[pl.ds(pl.multiple_of(c * width, width) + j * LANES, LANES), :] = low[
                :, j * LANES : (j + 1) * LANES
            ].T
        return 0

    lookups = entries // width
    early = lookups - (steps - 1)
    lax.fori_loop(0, early, lookup, 0)

    def edges_ready(t):
        for s, x, inward, buffer in ((0, 0, 1, send_lo), (1, across - 1, -1, send_hi)):
            v = [buffer[t, pl.ds(b * layers, layers), :] for b in range(nyb)]
            right = [pltpu.roll(u, LANES - 1, 1) for u in v]
            left = [pltpu.roll(u, 1, 1) for u in v]
            for b in range(nyb):
                own = pl.ds(b * layers, layers)
                y_up = jnp.where(lane_e == LANES - 1, right[min(b + 1, nyb - 1)], right[b])
                y_down = jnp.where(lane_e == 0, left[max(b - 1, 0)], left[b])
                inner = fields[t, pl.ds(slab + b * across + x + inward, layers, stride=slab), :]
                buffer[t + 1, own, :] = (
                    (rim[s, 0, own, :] * v[b] + rim[s, 1, own, :] * y_up)
                    + (rim[s, 2, own, :] * y_down + rim[s, 3, own, :] * inner)
                ) + (
                    (rim[s, 4, own, :] * pltpu.roll(v[b], layers - 1, 0)
                     + rim[s, 5, own, :] * pltpu.roll(v[b], 1, 0))
                    + mis[t, pl.ds(b * across + x, layers, stride=slab), :]
                )

    def edges_done(t):
        whole = pl.ds(0, edge)
        for s, arrived, buffer in ((0, from_lo, send_lo), (1, from_hi, send_hi)):
            buffer[t + 1, whole, :] = buffer[t + 1, whole, :] + rim[s, 6, :, :] * (
                arrived[t, whole, :] - buffer[t, whole, :]
            )

    def interior(t, last):
        def body(k, _):
            base = pl.multiple_of(k * slab, slab)
            def load(b):
                u = fields[t, pl.ds(base + slab + b * across, across), :]
                return u, pltpu.roll(u, LANES - 1, 1), pltpu.roll(u, 1, 1)

            here, right, left = load(0)
            left_before = left
            for b in range(nyb):
                own = pl.ds(base + b * across, across)
                following = load(b + 1) if b + 1 < nyb else (here, right, left)
                y_up = jnp.where(lane == LANES - 1, following[1], right)
                y_down = jnp.where(lane == 0, left_before, left)
                x_up = jnp.where(
                    sub == across - 1,
                    from_hi[t, pl.ds(b * layers + k, 1), :],
                    pltpu.roll(here, across - 1, 0),
                )
                x_down = jnp.where(
                    sub == 0, from_lo[t, pl.ds(b * layers + k, 1), :], pltpu.roll(here, 1, 0)
                )
                z_up = fields[t, pl.ds(base + 2 * slab + b * across, across), :]
                z_down = fields[t, own, :]
                new = (
                    (c0[own, :] * here + gyp[own, :] * y_up)
                    + (gym[own, :] * y_down + gxp[own, :] * (x_up - here))
                ) + (
                    (gxm[own, :] * (x_down - here)
                     + gz[pl.ds(base + slab + b * across, across), :] * z_up)
                    + (gz[own, :] * z_down + mis[t, own, :])
                )
                if last:
                    final[own, :] = new
                    acc = new
                    for s in range(1, steps):
                        acc = acc + fields[s, pl.ds(base + slab + b * across, across), :]
                    total[pl.ds(base + b, across, stride=nyb), :] = acc
                else:
                    fields[t + 1, pl.ds(base + slab + b * across, across), :] = new
                left_before = left
                here, right, left = following
            return 0

        lax.fori_loop(0, layers, body, 0)

    loads[0].wait()
    edges_ready(0)
    receive(0)
    for s, x, ref, arrived, outside in (
        (0, 0, gxm, from_lo, me == 0),
        (1, across - 1, gxp, from_hi, me == n - 1),
    ):
        scale = jnp.where(outside, 0.0, half)
        pair = scale * (
            packed[pl.ds(x, layers, stride=across), :] + arrived[0, pl.ds(edge, layers), :]
        )
        for b in range(nyb):
            value = jnp.broadcast_to(pair[:, b : b + 1], (layers, LANES))
            ref[pl.ds(b * across + x, layers, stride=slab), :] = value
            rim[s, 6, pl.ds(b * layers, layers), :] = value

    for t in range(steps):
        last = t == steps - 1
        if t > 0:
            loads[t].wait()
            if not last:
                edges_ready(t)
            receive(t)
        if not last:
            edges_done(t)
            send(t + 1)
        interior(t, last)
        if not last:
            lookup(early + t, 0)

    store = pltpu.make_async_copy(final, adjoint, sem_out)
    store.start()
    load_prof.wait()

    unroll = 32

    def pick(c, _):
        base = pl.multiple_of(c * unroll, unroll)
        for j in range(unroll):
            picked[pl.ds(base + j, 1), :] = total[pl.ds(block[base + j], 1), :]
        return 0

    lax.fori_loop(0, entries // unroll, pick, 0)

    chunk = 512
    sums = jnp.zeros((n * pad_rows, 3 * LANES), jnp.float32)
    for c in range(entries // chunk):
        own = pl.ds(c * chunk, chunk)
        value = DT * jnp.sum(
            picked[own, :] * prof[own, :], axis=1, keepdims=True
        )
        spread = one_lo[own, :] * value
        first = spread.astype(jnp.bfloat16)
        rest = spread - first.astype(jnp.float32)
        second = rest.astype(jnp.bfloat16)
        third = (rest - second.astype(jnp.float32)).astype(jnp.bfloat16)
        sums = sums + jnp.dot(
            one_hi[:, c * chunk : (c + 1) * chunk],
            jnp.concatenate([first, second, third], axis=1),
            preferred_element_type=jnp.float32,
        )
    dense[...] = (
        (sums[:, 2 * LANES :] + sums[:, LANES : 2 * LANES]) + sums[:, :LANES]
    ).reshape(n, pad_rows, LANES)

    def deliver(d):
        peer = lax.rem(me + d, n)
        return pltpu.make_async_remote_copy(
            src_ref=dense.at[peer],
            dst_ref=parts.at[d],
            send_sem=out_sems.at[d],
            recv_sem=in_sems.at[d],
            device_id={"gx": peer},
            device_id_type=MESH,
        )

    def start(d, _):
        deliver(d).start()
        return 0

    lax.fori_loop(1, n, start, 0, unroll=n <= 16)

    for t in range(steps):
        @pl.when(me < n - 1)
        def _():
            hop(t, True).wait_send()

        @pl.when(me > 0)
        def _():
            hop(t, False).wait_send()

    def finish(d, acc):
        deliver(d).wait_recv()
        return acc + parts[d]

    store.wait()
    result = lax.fori_loop(1, n, finish, dense[me], unroll=n <= 16)
    grad[...] = result[:owner_rows]

    def drain(d, _):
        deliver(d).wait_send()
        return 0

    lax.fori_loop(1, n, drain, 0, unroll=n <= 16)


PARTS = 4


def hand_on(adjoint_in, grad_in, adjoint, grad, held, held_grad, sems):
    size = adjoint.shape[0] // PARTS
    moves = [(grad_in, held_grad, grad)]
    for p in range(PARTS):
        part = pl.ds(p * size, size)
        moves.append((adjoint_in.at[part], held.at[part], adjoint.at[part]))
    loads = [pltpu.make_async_copy(a, b, sems.at[i, 0]) for i, (a, b, _) in enumerate(moves)]
    stores = [pltpu.make_async_copy(b, c, sems.at[i, 1]) for i, (_, b, c) in enumerate(moves)]
    for load in loads:
        load.start()
    for load, store in zip(loads, stores):
        load.wait()
        store.start()
    for store in stores:
        store.wait()


def on_device(
    terminal, misfit, material, material_table, heater_slot, entry_heater, entry_block, profile
):
    n = lax.axis_size("gx")
    layers, across, depth = terminal.shape
    steps = misfit.shape[0]
    mats = material_table.shape[1]
    nyb = depth // LANES
    entries = entry_block.shape[0]
    per_owner = heater_slot.shape[0] // n
    rows, slab, edge = layers * across * nyb, across * nyb, layers * nyb
    pad_rows = ceil8(per_owner // LANES)
    term = terminal.reshape(layers, across, nyb, LANES).swapaxes(1, 2).reshape(rows, LANES)
    mis = (
        misfit.reshape(steps, layers, across, nyb, LANES).swapaxes(2, 3).reshape(steps, rows, LANES)
    )
    hbm = pl.BlockSpec(memory_space=pltpu.HBM)
    vmem = pl.BlockSpec(memory_space=pltpu.VMEM)
    f32 = jnp.float32
    adjoint, grad = pl.pallas_call(
        functools.partial(kernel, n, layers, across, nyb, steps, mats, per_owner),
        out_shape=(
            jax.ShapeDtypeStruct((rows, LANES), f32),
            jax.ShapeDtypeStruct((per_owner // LANES, LANES), f32),
        ),
        in_specs=[hbm] * 8,
        out_specs=(hbm, vmem),
        scratch_shapes=[
            pltpu.VMEM((layers * across, nyb), jnp.int32),
            pltpu.SMEM(material_table.shape, f32),
            pltpu.VMEM((heater_slot.shape[0] // LANES, LANES), jnp.int32),
            pltpu.VMEM((entries // LANES, LANES), jnp.int32),
            pltpu.SMEM((entries,), jnp.int32),
            pltpu.VMEM((steps, rows + 2 * slab, LANES), f32),
            pltpu.VMEM((steps, rows, LANES), f32),
            pltpu.VMEM((entries, LANES), f32),
            pltpu.VMEM((rows, LANES), f32),
            pltpu.VMEM((rows, LANES), f32),
            pltpu.VMEM((rows, LANES), f32),
            pltpu.VMEM((rows, LANES), f32),
            pltpu.VMEM((rows + slab, LANES), f32),
            pltpu.VMEM((rows, LANES), f32),
            pltpu.VMEM((2, 7, edge, LANES), f32),
            pltpu.VMEM((layers * across, LANES), f32),
            pltpu.VMEM((layers * across, LANES), f32),
            pltpu.VMEM((rows, LANES), f32),
            pltpu.VMEM((entries, LANES), f32),
            pltpu.VMEM((rows, LANES), f32),
            pltpu.VMEM((entries, LANES), f32),
            pltpu.VMEM((n * pad_rows, entries), jnp.bfloat16),
            pltpu.VMEM((n, pad_rows, LANES), f32),
            pltpu.VMEM((steps, edge + layers, LANES), f32),
            pltpu.VMEM((steps, edge + layers, LANES), f32),
            pltpu.VMEM((steps, edge + layers, LANES), f32),
            pltpu.VMEM((steps, edge + layers, LANES), f32),
            pltpu.VMEM((n, pad_rows, LANES), f32),
            pltpu.SemaphoreType.DMA,
            pltpu.SemaphoreType.DMA((steps,)),
            pltpu.SemaphoreType.DMA,
            pltpu.SemaphoreType.DMA((5,)),
            pltpu.SemaphoreType.DMA((steps, 2)),
            pltpu.SemaphoreType.DMA((steps, 2)),
            pltpu.SemaphoreType.DMA((n,)),
            pltpu.SemaphoreType.DMA((n,)),
            pltpu.SemaphoreType.DMA,
        ],
        compiler_params=pltpu.CompilerParams(
            collective_id=0, has_side_effects=True, vmem_limit_bytes=64 * 1024 * 1024
        ),
    )(
        term,
        mis,
        material.reshape(layers * across, nyb),
        material_table,
        heater_slot.reshape(-1, LANES),
        entry_heater.reshape(-1, LANES),
        entry_block,
        profile,
    )
    adjoint, grad = pl.pallas_call(
        hand_on,
        out_shape=(
            jax.ShapeDtypeStruct(adjoint.shape, f32),
            jax.ShapeDtypeStruct(grad.shape, f32),
        ),
        in_specs=[hbm] * 2,
        out_specs=(hbm, hbm),
        scratch_shapes=[
            pltpu.VMEM(adjoint.shape, f32),
            pltpu.VMEM(grad.shape, f32),
            pltpu.SemaphoreType.DMA((PARTS + 1, 2)),
        ],
        compiler_params=pltpu.CompilerParams(vmem_limit_bytes=60 * 1024 * 1024),
    )(adjoint, grad)
    adjoint = adjoint.reshape(layers, nyb, across, LANES).swapaxes(1, 2).reshape(terminal.shape)
    return (adjoint, grad.reshape(per_owner))


def solution(mesh):
    return jax.shard_map(
        on_device,
        mesh=mesh,
        in_specs=(
            P("groups", "gx", None),
            P(None, "groups", "gx", None),
            P(None, "gx", None),
            P(),
            P(),
            P("gx"),
            P("gx"),
            P("gx", None),
        ),
        out_specs=(P("groups", "gx", None), P(("groups", "gx"))),
        check_vma=False,
    )
```
